32 devices in a mesh: group: 2 (over x), ctx: 16 (over z, y, core).
Axes of the slice: x: 2, y: 2, z: 4, core: 2. Of those that a mesh axis runs over, the one named last changes fastest.
Arguments:
- hyena_qkv: bfloat16 [4096, 3, 2048], P(('group', 'ctx')), parts along dimension 0, may hold values from -6 to 6
- short_weight: float32 [3, 3, 2048], replicated, may hold values from -3.5 to 3.5
- filter_rate: float32 [128, 16], replicated, as said below
- filter_residue: float32 [128, 16], replicated, may hold values from -4 to 4
- attn_qkv: bfloat16 [4096, 3, 2048], P(('group', 'ctx')), parts along dimension 0, may hold values from -6 to 6
- doc_lengths: int32 [8], P('group'), parts along dimension 0, may hold values from 1 to 897, 2048 in all
Outputs:
- hyena_out: bfloat16 [4096, 2048], P(('group', 'ctx')), parts along dimension 0
- attn_out: bfloat16 [4096, 2048], P(('group', 'ctx')), parts along dimension 0
The draws below stay inside these ranges and needn't reach their ends.
There are 2 independent parts, one for each index of `group`. The reference program is written for one: setup_inputs(seed, part) draws one part's arguments, and reference() takes and returns one part's arrays. A program takes and returns all parts, laid end to end along the dimension named above; an argument that names none is the same for every part. Nothing has to cross between parts.
Inputs may be any that keep to these rules, and one draw needn't show every extreme that they name: `filter_rate`: every rate is positive and at most 1/30. `doc_lengths`: the lengths sum to 2048 and the longest is exactly 897.
All inputs are finite; a program needn't handle non-finite values.
Results may differ from the reference program's by a relative error of at most 0.0054.
Values may be sent and summed in bfloat16 or wider, within the bound.
A program may use at most 128 MiB of HBM per device.

```python
import math
import jax
import jax.numpy as jnp
import numpy as np
from jax import lax

TOK_DEV = 128
HEAD = 128
MODES = 16
SPAN = 8
CHAN = 2048
FILTERS = 128
TOKENS = 2048
MOST = 897
DOCS = 4


def draw_filter_rate(key, part):
    key_slow, key_fast, key_pick = jax.random.split(key, 3)
    shape = (FILTERS, MODES)
    rate_slow = jnp.exp(jax.random.uniform(key_slow, shape, jnp.float32, math.log(0.2), 0.0)) * (math.log(10.0) / TOKENS)
    rate_fast = jax.random.uniform(key_fast, shape, jnp.float32, 1.0 / 50.0, 1.0 / 30.0)
    share_fast = 0.5
    picked = jax.random.uniform(key_pick, shape, jnp.float32) < share_fast
    return jnp.where(picked, rate_fast, rate_slow)


def draw_attn_qkv(key, part):
    drawn = jnp.clip(jax.random.normal(key, (TOKENS, 3, CHAN), jnp.float32), -4.0, 4.0)
    return drawn.astype(jnp.bfloat16)


def level_of(own_key, extent, shards, low, high):
    def one(axis_at, shards_of):
        steps = jax.random.uniform(jax.random.fold_in(jax.random.fold_in(own_key, 6), axis_at), (shards_of,), jnp.float32, low / len(shards), high / len(shards))
        return jnp.repeat(jnp.exp(steps), extent[axis_at] // shards_of).reshape((-1,) + (1,) * (len(extent) - axis_at - 1))

    loudness = one(*shards[0])
    for cut in shards[1:]:
        loudness = loudness * one(*cut)
    return loudness


def profile(amount, total, most, slope):
    weights = [(1 << 20) // math.isqrt(standing ** slope) + 1 for standing in range(2, amount + 1)]
    spare, given = total - most - (amount - 1), [1] * (amount - 1)
    while spare > 0:
        movable = [i for i in range(amount - 1) if given[i] < most]
        pool, budget = sum([weights[i] for i in movable]), spare
        for i in movable:
            addition = min(most - given[i], max(1, budget * weights[i] // pool), spare)
            given[i] = given[i] + addition
            spare = spare - addition
    return np.array([most] + given)


def ragged_sizes(own_key, amount, total, bound, slope):
    if amount == 2:
        one = jax.random.randint(own_key, (), max(1, total - bound), min(bound, total - 1) + 1)
        return jnp.stack([one, total - one])
    lengths = jnp.asarray(profile(amount, total, bound, slope), jnp.int32)
    twos = (amount - 1) // 2
    donor, taker = lengths[1:1 + 2 * twos:2], lengths[2:2 + 2 * twos:2]
    slack = jnp.minimum(donor - 1, bound - taker)
    passed = jax.random.randint(jax.random.fold_in(own_key, 1), (twos,), 0, 1 << 20) % (slack + 1)
    lengths = lengths.at[1:1 + 2 * twos:2].set(donor - passed).at[2:2 + 2 * twos:2].set(taker + passed)
    return lengths[jax.random.permutation(jax.random.fold_in(own_key, 2), amount)]


def bell_draw(stream_key, shape, scale, limit, pieces=(), held_as=jnp.bfloat16):
    factor_of = level_of(stream_key, shape, pieces, -0.22, 0.18) if pieces else 1.0
    entries = jax.random.normal(stream_key, shape, jnp.float32) * scale * factor_of
    return jnp.minimum(jnp.maximum(entries, -limit), limit).astype(held_as)


def setup_inputs(seed: int = 0, part: int = 0) -> dict:
    arg_keys = jax.random.split(jax.random.key(seed), 7)
    part_keys = jax.random.split(jax.random.fold_in(arg_keys[6], part), 7)
    return {
        "hyena_qkv": bell_draw(part_keys[0], (TOKENS, 3, CHAN), 1.0, 6.0, ((0, 16),)),
        "short_weight": bell_draw(arg_keys[1], (3, 3, CHAN), 3 ** -0.5, 3.5, (), jnp.float32),
        "filter_rate": draw_filter_rate(jax.random.fold_in(arg_keys[6], 71), part),
        "filter_residue": bell_draw(arg_keys[3], (FILTERS, MODES), 1.0, 4.0, (), jnp.float32),
        "attn_qkv": draw_attn_qkv(jax.random.fold_in(jax.random.fold_in(arg_keys[6], part), 71), part),
        "doc_lengths": ragged_sizes(part_keys[5], DOCS, TOKENS, MOST, 2).astype(jnp.int32),
    }


precise = lax.Precision.HIGHEST

def featurize(token_rows, before, short_weight):
    row_count = token_rows.shape[0]
    padded = jnp.concatenate([before, token_rows], axis=0).astype(jnp.float32)
    return short_weight[0] * padded[2:] + short_weight[1] * padded[1:row_count + 1] + short_weight[2] * padded[:row_count]

def filter_terms(filter_rate, filter_residue, row_count):
    mode_coeff = filter_residue * jnp.sqrt(2.0 * filter_rate / filter_rate.shape[1])
    lag_values = jnp.arange(row_count).astype(jnp.float32)
    powers = jnp.exp(-filter_rate[:, :, None] * lag_values)
    filter_taps = jnp.einsum('gm,gmk->gk', mode_coeff, powers, precision=precise)
    return (mode_coeff, filter_taps.astype(jnp.bfloat16))

def toeplitz(filter_taps):
    row_count = filter_taps.shape[1]
    lag_index = jnp.arange(row_count, dtype=jnp.int32)[:, None] - jnp.arange(row_count, dtype=jnp.int32)[None, :]
    lag_table = jnp.take(filter_taps, jnp.clip(lag_index, 0, row_count - 1), axis=1)
    return jnp.where(lag_index[None] >= 0, lag_table, jnp.zeros((), filter_taps.dtype))

def block_ends(mixed_in, filter_rate):
    row_count, channels = mixed_in.shape
    groups = filter_rate.shape[0]
    lag_values = (row_count - 1 - jnp.arange(row_count)).astype(jnp.float32)
    powers = jnp.exp(-filter_rate[:, :, None] * lag_values)
    grouped = mixed_in.astype(jnp.float32).reshape(row_count, groups, channels // groups)
    return jnp.einsum('gms,sgc->gmc', powers, grouped, precision=precise)

def block_far(carried, filter_rate, mode_coeff, row_count):
    lag_values = jnp.arange(1, row_count + 1).astype(jnp.float32)
    powers = mode_coeff[:, :, None] * jnp.exp(-filter_rate[:, :, None] * lag_values)
    return jnp.einsum('gmt,gmc->tgc', powers, carried, precision=precise)

def visible(query_pos, key_pos, doc_lengths):
    bounds = jnp.cumsum(doc_lengths, dtype=jnp.int32)
    query_doc = lax.optimization_barrier(jnp.sum((query_pos[:, None] >= bounds[None, :]).astype(jnp.int32), axis=1))
    key_doc = lax.optimization_barrier(jnp.sum((key_pos[:, None] >= bounds[None, :]).astype(jnp.int32), axis=1))
    causal = (key_pos[None, :] <= query_pos[:, None]) & (key_pos[None, :] >= 0)
    return causal & (key_doc[None, :] == query_doc[:, None])

def attend(queries, keys, values, allowed):
    row_count, channels = queries.shape
    heads = channels // HEAD

    def split_heads(matrix):
        return matrix.reshape(matrix.shape[0], heads, HEAD).transpose(1, 0, 2)

    def one_head(head_parts):
        query_rows, key_rows, value_rows = head_parts
        scores = jnp.dot(query_rows, key_rows.T, preferred_element_type=jnp.float32) * (1.0 / math.sqrt(HEAD))
        scores = jnp.where(allowed, scores, -jnp.inf)
        row_max = lax.optimization_barrier(jnp.max(scores, axis=1, keepdims=True))
        exp_scores = jnp.exp(scores - row_max)
        weight = (exp_scores / lax.optimization_barrier(jnp.sum(exp_scores, axis=1, keepdims=True))).astype(jnp.bfloat16)
        return jnp.dot(weight, value_rows, preferred_element_type=jnp.float32).astype(jnp.bfloat16)
    head_out = lax.map(one_head, (split_heads(queries), split_heads(keys), split_heads(values)))
    return head_out.transpose(1, 0, 2).reshape(row_count, channels)

def reference(hyena_qkv, short_weight, filter_rate, filter_residue, attn_qkv, doc_lengths):
    block_count = TOKENS // TOK_DEV
    groups = filter_rate.shape[0]
    mode_coeff, filter_taps = filter_terms(filter_rate, filter_residue, TOK_DEV)
    toeplitz_taps = toeplitz(filter_taps).astype(jnp.float32)
    block_decay = jnp.exp(-filter_rate * TOK_DEV)

    def advance(state, token_rows):
        carried, before = state
        featured = featurize(token_rows, before, short_weight)
        mixed_in = (featured[:, 1] * featured[:, 2]).astype(jnp.bfloat16)
        grouped = mixed_in.astype(jnp.float32).reshape(TOK_DEV, groups, CHAN // groups)
        near_part = jnp.einsum('gts,sgc->tgc', toeplitz_taps, grouped, precision=precise)
        far_part = block_far(carried, filter_rate, mode_coeff, TOK_DEV)
        mixed_out = (featured[:, 0] * (near_part + far_part).reshape(TOK_DEV, CHAN)).astype(jnp.bfloat16)
        carried = block_decay[:, :, None] * carried + block_ends(mixed_in, filter_rate)
        return ((carried, token_rows[TOK_DEV - 2:]), mixed_out)
    zero_state = jnp.zeros((groups, MODES, CHAN // groups), jnp.float32)
    opening = jnp.zeros((2, 3, CHAN), jnp.bfloat16)
    _, block_outs = lax.scan(advance, (zero_state, opening), hyena_qkv.reshape(block_count, TOK_DEV, 3, CHAN))
    hyena_out = block_outs.reshape(TOKENS, CHAN)
    all_queries = attn_qkv[:, 0]
    padding = jnp.zeros(((SPAN - 1) * TOK_DEV, 2, CHAN), jnp.bfloat16)
    padded = jnp.concatenate([padding, attn_qkv[:, 1:]], axis=0)

    def one_block(block_id):
        first_row = block_id * TOK_DEV
        queries = lax.dynamic_slice_in_dim(all_queries, first_row, TOK_DEV, 0)
        window = lax.dynamic_slice_in_dim(padded, first_row, SPAN * TOK_DEV, 0)
        query_pos = first_row + jnp.arange(TOK_DEV, dtype=jnp.int32)
        key_pos = first_row - (SPAN - 1) * TOK_DEV + jnp.arange(SPAN * TOK_DEV, dtype=jnp.int32)
        allowed = visible(query_pos, key_pos, doc_lengths)
        return attend(queries, window[:, 0], window[:, 1], allowed)
    attn_out = lax.map(one_block, jnp.arange(block_count, dtype=jnp.int32)).reshape(TOKENS, CHAN)
    return (hyena_out, attn_out)
```

```python
import functools
import math

import jax
import jax.numpy as jnp
from jax import lax
from jax.experimental import pallas as pl
from jax.experimental.pallas import tpu as pltpu
from jax.sharding import PartitionSpec as P

HEAD = 128
SPAN = 8


precise = lax.Precision.HIGHEST


def from_behind(value, axis, steps):
    count = lax.axis_size(axis)
    initial, last = (max(0, -steps), min(count, count - steps))
    return lax.ppermute(value, axis, [(source, source + steps) for source in range(initial, last)])


def featurize(token_rows, before, short_weight):
    row_count = token_rows.shape[0]
    padded = jnp.concatenate([before, token_rows], axis=0).astype(jnp.float32)
    return (
        short_weight[0] * padded[2:]
        + short_weight[1] * padded[1 : row_count + 1]
        + short_weight[2] * padded[:row_count]
    )


def filter_terms(filter_rate, filter_residue, row_count):
    mode_coeff = filter_residue * jnp.sqrt(2.0 * filter_rate / filter_rate.shape[1])
    lag_values = jnp.arange(row_count).astype(jnp.float32)
    powers = jnp.exp(-filter_rate[:, :, None] * lag_values)
    filter_taps = jnp.einsum("gm,gmk->gk", mode_coeff, powers, precision=precise)
    return (mode_coeff, filter_taps.astype(jnp.bfloat16))


def toeplitz(filter_taps):
    row_count = filter_taps.shape[1]
    lag_index = (
        jnp.arange(row_count, dtype=jnp.int32)[:, None]
        - jnp.arange(row_count, dtype=jnp.int32)[None, :]
    )
    lag_table = jnp.take(filter_taps, jnp.clip(lag_index, 0, row_count - 1), axis=1)
    return jnp.where(lag_index[None] >= 0, lag_table, jnp.zeros((), filter_taps.dtype))


def block_ends(mixed_in, filter_rate):
    row_count, channels = mixed_in.shape
    groups = filter_rate.shape[0]
    lag_values = (row_count - 1 - jnp.arange(row_count)).astype(jnp.float32)
    powers = jnp.exp(-filter_rate[:, :, None] * lag_values)
    grouped = mixed_in.astype(jnp.float32).reshape(row_count, groups, channels // groups)
    return jnp.einsum("gms,sgc->gmc", powers, grouped, precision=precise)


def block_far(carried, filter_rate, mode_coeff, row_count):
    lag_values = jnp.arange(1, row_count + 1).astype(jnp.float32)
    powers = mode_coeff[:, :, None] * jnp.exp(-filter_rate[:, :, None] * lag_values)
    return jnp.einsum("gmt,gmc->tgc", powers, carried, precision=precise)


def visible(query_pos, key_pos, doc_lengths):
    docs = doc_lengths.shape[0]
    upto = jnp.arange(docs)[:, None] >= jnp.arange(docs)[None, :]
    bounds = jnp.sum(jnp.where(upto, doc_lengths[None, :], 0), axis=1)
    query_doc = jnp.sum((query_pos[:, None] >= bounds[None, :]).astype(jnp.int32), axis=1)
    key_doc = jnp.sum((key_pos[:, None] >= bounds[None, :]).astype(jnp.int32), axis=1)
    causal = (key_pos[None, :] <= query_pos[:, None]) & (key_pos[None, :] >= 0)
    return causal & (key_doc[None, :] == query_doc[:, None])


def attend(queries, keys, values, allowed):
    row_count, channels = queries.shape
    heads = channels // HEAD

    def split_heads(matrix):
        return matrix.reshape(matrix.shape[0], heads, HEAD).transpose(1, 0, 2)

    def one_head(head_parts):
        query_rows, key_rows, value_rows = head_parts
        scores = jnp.dot(query_rows, key_rows.T, preferred_element_type=jnp.float32) * (
            1.0 / math.sqrt(HEAD)
        )
        scores = jnp.where(allowed, scores, -jnp.inf)
        row_max = jnp.max(scores, axis=1, keepdims=True)
        exp_scores = jnp.exp(scores - row_max)
        weight = (exp_scores / jnp.sum(exp_scores, axis=1, keepdims=True)).astype(jnp.bfloat16)
        return jnp.dot(weight, value_rows, preferred_element_type=jnp.float32).astype(jnp.bfloat16)

    head_out = lax.map(one_head, (split_heads(queries), split_heads(keys), split_heads(values)))
    return head_out.transpose(1, 0, 2).reshape(row_count, channels)


def on_device(hyena_qkv, short_weight, filter_rate, filter_residue, attn_qkv, doc_lengths):
    row_count = hyena_qkv.shape[0]
    channels = hyena_qkv.shape[2]
    groups = filter_rate.shape[0]
    device_index = lax.axis_index("ctx")
    before = from_behind(hyena_qkv[row_count - 2 :], "ctx", 1)
    featured = featurize(hyena_qkv, before, short_weight)
    mixed_in = (featured[:, 1] * featured[:, 2]).astype(jnp.bfloat16)
    mode_coeff, filter_taps = filter_terms(filter_rate, filter_residue, row_count)
    grouped = mixed_in.reshape(row_count, groups, channels // groups)
    near_part = jnp.einsum(
        "gts,sgc->tgc", toeplitz(filter_taps), grouped, preferred_element_type=jnp.float32
    )
    end_states = block_ends(mixed_in, filter_rate)
    pieces = lax.all_gather(end_states[None], "ctx", axis=0, tiled=True)
    owners = jnp.arange(pieces.shape[0], dtype=jnp.int32)
    absorb_distance = device_index - 1 - owners
    lag_values = (jnp.maximum(absorb_distance, 0) * row_count).astype(jnp.float32)
    powers = jnp.exp(-filter_rate[None] * lag_values[:, None, None])
    powers = jnp.where((absorb_distance >= 0)[:, None, None], powers, 0.0)
    carried = jnp.einsum("ngm,ngmc->gmc", powers, pieces, precision=precise)
    far_part = block_far(carried, filter_rate, mode_coeff, row_count)
    hyena_out = (featured[:, 0] * (near_part + far_part).reshape(row_count, channels)).astype(
        jnp.bfloat16
    )
    key_pairs = attn_qkv[:, 1:]
    key_blocks = [key_pairs]
    moving = key_pairs
    for distance in range(1, SPAN):
        moving = from_behind(moving, "ctx", 1)
        key_blocks.append(moving)
    window = jnp.concatenate(key_blocks[::-1], axis=0)
    query_pos = device_index * row_count + jnp.arange(row_count, dtype=jnp.int32)
    key_pos = (device_index - SPAN + 1) * row_count + jnp.arange(SPAN * row_count, dtype=jnp.int32)
    allowed = visible(query_pos, key_pos, doc_lengths)
    attn_out = attend(attn_qkv[:, 0], window[:, 0], window[:, 1], allowed)
    return (hyena_out, attn_out)


LANES = 128
PLANE = 4
EDGE = 16


def fused_kernel(
    n,
    hq,
    short_weight,
    rate_t,
    residue_t,
    docs,
    aq,
    hyena_out,
    attn_out,
    gath,
    obuf,
    prev,
    query,
    near,
    far_powers,
    rate_c,
    own_state,
    state_send,
    state_in,
    total_send,
    total_in,
    sem_q_send,
    sem_q_recv,
    sem_o_send,
    sem_o_recv,
    sem_edge,
    sem_s_send,
    sem_s_recv,
    sem_t_send,
    sem_t_recv,
):
    rows = hq.shape[1]
    modes = rate_t.shape[0]
    groups = rate_t.shape[1]
    channels = hq.shape[2]
    width = channels // groups
    per_tile = LANES // width
    tiles = channels // LANES
    planes = n // PLANE
    me = lax.axis_index("ctx")
    plane = me // PLANE
    spot = lax.rem(me, PLANE)

    def remote(src, dst, send_sem, recv_sem, target):
        return pltpu.make_async_remote_copy(
            src_ref=src,
            dst_ref=dst,
            send_sem=send_sem,
            recv_sem=recv_sem,
            device_id={"ctx": target},
            device_id_type=pl.DeviceIdType.MESH,
        )

    def head_columns(h):
        return pl.ds(pl.multiple_of(h * HEAD, HEAD), HEAD)

    def send_head(h, slot):
        return remote(
            aq.at[:, :, head_columns(h)],
            gath.at[slot],
            sem_q_send.at[h],
            sem_q_recv.at[slot],
            h,
        )

    def send_out(b, slot):
        return remote(
            obuf.at[b],
            attn_out.at[:, head_columns(slot)],
            sem_o_send.at[b],
            sem_o_recv.at[slot],
            b,
        )

    def send_edge():
        return remote(
            hq.at[:, pl.ds(rows - EDGE, EDGE), :],
            prev,
            sem_edge.at[0],
            sem_edge.at[1],
            lax.rem(me + 1, n),
        )

    def send_state(target_spot, slot):
        return remote(
            state_send,
            state_in.at[slot],
            sem_s_send.at[target_spot],
            sem_s_recv.at[slot],
            plane * PLANE + target_spot,
        )

    def send_total(target_plane, slot):
        return remote(
            total_send,
            total_in.at[slot],
            sem_t_send.at[target_plane],
            sem_t_recv.at[slot],
            target_plane * PLANE + spot,
        )

    barrier = pltpu.get_barrier_semaphore()

    @pl.loop(1, n)
    def _(k):
        pl.semaphore_signal(
            barrier,
            inc=1,
            device_id={"ctx": lax.rem(me + k, n)},
            device_id_type=pl.DeviceIdType.MESH,
        )

    pl.semaphore_wait(barrier, n - 1)

    @pl.when(me < n - 1)
    def _():
        send_edge().start()

    @pl.loop(1, n)
    def _(k):
        send_head(lax.rem(me + k, n), me).start()

    own_heads = pltpu.make_async_copy(
        aq.at[:, :, head_columns(me)], gath.at[me], sem_q_recv.at[me]
    )
    own_heads.start()

    @pl.when(me == 0)
    def _():
        prev[...] = jnp.zeros_like(prev)

    @pl.when(me > 0)
    def _():
        send_edge().wait_recv()

    lane = lax.broadcasted_iota(jnp.int32, (1, LANES), 1)
    sub = lax.broadcasted_iota(jnp.int32, (LANES, 1), 0)
    own_block = (sub // width) == (lane // width)
    row_col = lax.broadcasted_iota(jnp.int32, (rows, 1), 0)
    row_f = row_col.astype(jnp.float32)
    key_row = lax.broadcasted_iota(jnp.int32, (1, rows), 1)
    lower = key_row <= row_col
    mode_pick = lax.broadcasted_iota(jnp.int32, (modes, 1), 0) == lax.rem(lane, modes)
    rev_f = lax.rem(rows - row_col, rows).astype(jnp.float32)
    filter_of = (
        lax.broadcasted_iota(jnp.int32, (per_tile, 1), 0) == lane // width
    ).astype(jnp.float32)

    @pl.loop(0, tiles)
    def _(i):
        at = pl.ds(pl.multiple_of(i * LANES, LANES), LANES)

        def feature(j):
            value = jnp.concatenate([prev[j, :, at], hq[j, :, at]], axis=0).astype(jnp.float32)
            one = pltpu.roll(value, 1, 0)
            two = pltpu.roll(value, 2, 0)
            return (
                short_weight[0, pl.ds(j, 1), at] * value[EDGE:]
                + short_weight[1, pl.ds(j, 1), at] * one[EDGE:]
                + short_weight[2, pl.ds(j, 1), at] * two[EDGE:]
            )

        query[:, at] = feature(0)
        mixed_f = feature(1) * feature(2)
        mixed_b = mixed_f.astype(jnp.bfloat16)
        mixed_in = mixed_b.astype(jnp.float32)

        pick = (
            lax.broadcasted_iota(jnp.int32, (groups, LANES), 0)
            == i * per_tile + lane // width
        ).astype(jnp.float32)
        rates = jnp.dot(rate_t[...], pick, precision=precise, preferred_element_type=jnp.float32)
        residues = jnp.dot(
            residue_t[...], pick, precision=precise, preferred_element_type=jnp.float32
        )
        coeffs = residues * jnp.sqrt(2.0 * rates / modes)
        rate_c[:, at] = rates
        rate_row = jnp.sum(jnp.where(mode_pick, rates, 0.0), axis=0, keepdims=True)
        coeff_row = jnp.sum(jnp.where(mode_pick, coeffs, 0.0), axis=0, keepdims=True)

        ends = jnp.exp(-rate_row * (rows - 1 - row_f))
        full = lax.dot_general(
            ends,
            mixed_in,
            (((0,), (0,)), ((), ())),
            precision=precise,
            preferred_element_type=jnp.float32,
        )
        full = jnp.where(own_block, full, 0.0).reshape(per_tile, modes, LANES)
        state = jnp.sum(full, axis=0)
        own_state[:, at] = state
        state_send[:, at] = state.astype(jnp.bfloat16)
        far_powers[:, at] = coeff_row * jnp.exp(-rate_row * (row_f + 1.0))

        taps_powers = coeff_row * jnp.exp(-rate_row * rev_f)
        taps = lax.dot_general(
            filter_of,
            taps_powers,
            (((1,), (1,)), ((), ())),
            precision=precise,
            preferred_element_type=jnp.float32,
        )
        tables = []
        inputs = []
        for g in range(per_tile):
            spread = jnp.broadcast_to(taps[g : g + 1, :], (rows, rows))
            table = pltpu.roll(spread, 0, 1, stride=1, stride_axis=0)
            tables.append(jnp.where(lower, table, 0.0).astype(jnp.bfloat16))
            inputs.append(jnp.where(lane // width == g, mixed_in, 0.0).astype(jnp.bfloat16))
        near[:, at] = jnp.dot(
            jnp.concatenate(tables, axis=1),
            jnp.concatenate(inputs, axis=0),
            preferred_element_type=jnp.float32,
        )

    for other in range(PLANE):

        @pl.when(spot != other)
        def _(other=other):
            send_state(other, spot).start()

    def decay(steps):
        return jnp.exp(rate_c[...] * (-float(rows) * steps.astype(jnp.float32)))

    own_state[...] = decay(PLANE - 1 - spot) * own_state[...]
    for other in range(PLANE):

        @pl.when(spot != other)
        def _(other=other):
            send_state(other, other).wait_recv()
            own_state[...] += decay(jnp.int32(PLANE - 1 - other)) * state_in[other].astype(
                jnp.float32
            )

    total_send[...] = own_state[...].astype(jnp.bfloat16)
    for later in range(planes):

        @pl.when(plane < later)
        def _(later=later):
            send_total(later, plane).start()

    bounds = []
    running = jnp.int32(0)
    for k in range(docs.shape[0]):
        running = running + docs[k]
        bounds.append(running)
    scale = 1.0 / math.sqrt(HEAD)
    span = min(SPAN, n)
    head_row = lax.broadcasted_iota(jnp.int32, (rows, 1), 0)
    window_row = lax.broadcasted_iota(jnp.int32, (1, span * rows), 1)

    def wait_head(b):
        @pl.when(b != me)
        def _():
            send_head(b, b).wait_recv()

        @pl.when(b == me)
        def _():
            own_heads.wait()

    def attend_block(b):
        begin = jnp.maximum(b - (span - 1), 0)
        keys = gath[pl.ds(begin, span), 1].reshape(span * rows, HEAD)
        values = gath[pl.ds(begin, span), 2].reshape(span * rows, HEAD)
        scores = lax.dot_general(
            gath[b, 0], keys, (((1,), (1,)), ((), ())), preferred_element_type=jnp.float32
        )
        query_pos = b * rows + head_row
        first = jnp.zeros_like(query_pos)
        for bound in bounds:
            first = jnp.where(query_pos >= bound, bound, first)
        key_pos = begin * rows + window_row
        allowed = (key_pos <= query_pos) & (key_pos >= first)
        scores = jnp.where(allowed, scores, -jnp.inf)
        row_max = jnp.max(scores, axis=1, keepdims=True)
        exp_scores = jnp.exp((scores - row_max) * scale)
        row_sum = jnp.sum(exp_scores, axis=1, keepdims=True)
        mixed_values = jnp.dot(
            exp_scores.astype(jnp.bfloat16), values, preferred_element_type=jnp.float32
        )
        obuf[b] = (mixed_values / row_sum).astype(jnp.bfloat16)

        @pl.when(b != me)
        def _():
            send_out(b, me).start()

        @pl.when(b == me)
        def _():
            pltpu.make_async_copy(
                obuf.at[b], attn_out.at[:, head_columns(me)], sem_o_recv.at[me]
            ).start()

    @pl.loop(0, span)
    def _(b):
        wait_head(b)

    @pl.loop(0, span)
    def _(b):
        attend_block(b)

    @pl.loop(span, n)
    def _(b):
        wait_head(b)
        attend_block(b)

    own_state[...] = jnp.zeros(own_state.shape, jnp.float32)
    for earlier in range(planes):

        @pl.when(earlier < plane)
        def _(earlier=earlier):
            send_total(earlier, earlier).wait_recv()
            steps = PLANE * (plane - 1 - earlier) + spot
            own_state[...] += decay(steps) * total_in[earlier].astype(jnp.float32)

    for other in range(PLANE):

        @pl.when(other < spot)
        def _(other=other):
            own_state[...] += decay(spot - 1 - other) * state_in[other].astype(jnp.float32)

    @pl.loop(0, tiles)
    def _(i):
        at = pl.ds(pl.multiple_of(i * LANES, LANES), LANES)
        carried = jnp.concatenate([own_state[:, at]] * per_tile, axis=0)
        carried = jnp.where(own_block, carried, 0.0)
        far = jnp.dot(
            far_powers[:, at], carried, precision=precise, preferred_element_type=jnp.float32
        )
        hyena_out[:, at] = (query[:, at] * (near[:, at] + far)).astype(jnp.bfloat16)

    @pl.when(me < n - 1)
    def _():
        send_edge().wait_send()

    for other in range(PLANE):

        @pl.when(spot != other)
        def _(other=other):
            send_state(other, spot).wait_send()

    for later in range(planes):

        @pl.when(plane < later)
        def _(later=later):
            send_total(later, plane).wait_send()

    @pl.loop(0, n)
    def _(b):
        @pl.when(b != me)
        def _():
            send_head(b, me).wait_send()
            send_out(b, me).wait_send()
            send_out(b, b).wait_recv()

        @pl.when(b == me)
        def _():
            pltpu.make_async_copy(
                obuf.at[b], attn_out.at[:, head_columns(me)], sem_o_recv.at[me]
            ).wait()


def by_heads(n, hyena_qkv, short_weight, filter_rate, filter_residue, attn_qkv, doc_lengths):
    rows, streams, channels = hyena_qkv.shape
    modes = filter_rate.shape[1]
    out = jax.ShapeDtypeStruct((rows, channels), jnp.bfloat16)
    vmem = pl.BlockSpec(memory_space=pltpu.VMEM)
    dma = pltpu.SemaphoreType.DMA
    bf16, f32 = jnp.bfloat16, jnp.float32
    return pl.pallas_call(
        functools.partial(fused_kernel, n),
        out_shape=(out, out),
        in_specs=[vmem] * 4
        + [pl.BlockSpec(memory_space=pltpu.SMEM), pl.BlockSpec(memory_space=pl.ANY)],
        out_specs=(vmem, vmem),
        scratch_shapes=[
            pltpu.VMEM((n, streams, rows, HEAD), bf16),
            pltpu.VMEM((n, rows, HEAD), bf16),
            pltpu.VMEM((streams, EDGE, channels), bf16),
            pltpu.VMEM((rows, channels), f32),
            pltpu.VMEM((rows, channels), f32),
            pltpu.VMEM((rows, channels), f32),
            pltpu.VMEM((modes, channels), f32),
            pltpu.VMEM((modes, channels), f32),
            pltpu.VMEM((modes, channels), bf16),
            pltpu.VMEM((PLANE, modes, channels), bf16),
            pltpu.VMEM((modes, channels), bf16),
            pltpu.VMEM((n // PLANE, modes, channels), bf16),
            dma((n,)),
            dma((n,)),
            dma((n,)),
            dma((n,)),
            dma((2,)),
            dma((PLANE,)),
            dma((PLANE,)),
            dma((n // PLANE,)),
            dma((n // PLANE,)),
        ],
        compiler_params=pltpu.CompilerParams(
            collective_id=0, has_side_effects=True, vmem_limit_bytes=48 * 2**20
        ),
    )(
        hyena_qkv.transpose(1, 0, 2),
        short_weight,
        filter_rate.T,
        filter_residue.T,
        doc_lengths,
        attn_qkv.transpose(1, 0, 2),
    )


def on_any_slice(hyena_qkv, short_weight, filter_rate, filter_residue, attn_qkv, doc_lengths):
    n = lax.axis_size("ctx")
    rows, _, channels = hyena_qkv.shape
    groups, modes = filter_rate.shape
    fits = (
        channels == n * HEAD
        and n % PLANE == 0
        and channels == groups * modes
        and LANES % modes == 0
        and rows == LANES
    )
    args = (hyena_qkv, short_weight, filter_rate, filter_residue, attn_qkv, doc_lengths)
    return by_heads(n, *args) if fits else on_device(*args)


def solution(mesh):
    in_specs = (
        P(("group", "ctx"), None, None),
        P(),
        P(),
        P(),
        P(("group", "ctx"), None, None),
        P("group"),
    )
    out_specs = (P(("group", "ctx"), None), P(("group", "ctx"), None))
    return jax.shard_map(
        on_any_slice, mesh=mesh, in_specs=in_specs, out_specs=out_specs, check_vma=False
    )
```

```python
import functools
import math

import jax
import jax.numpy as jnp
from jax import lax
from jax.experimental import pallas as pl
from jax.experimental.pallas import tpu as pltpu
from jax.sharding import PartitionSpec as P

HEAD = 128
SPAN = 8


precise = lax.Precision.HIGHEST


def from_behind(value, axis, steps):
    count = lax.axis_size(axis)
    initial, last = (max(0, -steps), min(count, count - steps))
    return lax.ppermute(value, axis, [(source, source + steps) for source in range(initial, last)])


def featurize(token_rows, before, short_weight):
    row_count = token_rows.shape[0]
    padded = jnp.concatenate([before, token_rows], axis=0).astype(jnp.float32)
    return (
        short_weight[0] * padded[2:]
        + short_weight[1] * padded[1 : row_count + 1]
        + short_weight[2] * padded[:row_count]
    )


def filter_terms(filter_rate, filter_residue, row_count):
    mode_coeff = filter_residue * jnp.sqrt(2.0 * filter_rate / filter_rate.shape[1])
    lag_values = jnp.arange(row_count).astype(jnp.float32)
    powers = jnp.exp(-filter_rate[:, :, None] * lag_values)
    filter_taps = jnp.einsum("gm,gmk->gk", mode_coeff, powers, precision=precise)
    return (mode_coeff, filter_taps.astype(jnp.bfloat16))


def toeplitz(filter_taps):
    row_count = filter_taps.shape[1]
    lag_index = (
        jnp.arange(row_count, dtype=jnp.int32)[:, None]
        - jnp.arange(row_count, dtype=jnp.int32)[None, :]
    )
    lag_table = jnp.take(filter_taps, jnp.clip(lag_index, 0, row_count - 1), axis=1)
    return jnp.where(lag_index[None] >= 0, lag_table, jnp.zeros((), filter_taps.dtype))


def block_ends(mixed_in, filter_rate):
    row_count, channels = mixed_in.shape
    groups = filter_rate.shape[0]
    lag_values = (row_count - 1 - jnp.arange(row_count)).astype(jnp.float32)
    powers = jnp.exp(-filter_rate[:, :, None] * lag_values)
    grouped = mixed_in.astype(jnp.float32).reshape(row_count, groups, channels // groups)
    return jnp.einsum("gms,sgc->gmc", powers, grouped, precision=precise)


def block_far(carried, filter_rate, mode_coeff, row_count):
    lag_values = jnp.arange(1, row_count + 1).astype(jnp.float32)
    powers = mode_coeff[:, :, None] * jnp.exp(-filter_rate[:, :, None] * lag_values)
    return jnp.einsum("gmt,gmc->tgc", powers, carried, precision=precise)


def visible(query_pos, key_pos, doc_lengths):
    docs = doc_lengths.shape[0]
    upto = jnp.arange(docs)[:, None] >= jnp.arange(docs)[None, :]
    bounds = jnp.sum(jnp.where(upto, doc_lengths[None, :], 0), axis=1)
    query_doc = jnp.sum((query_pos[:, None] >= bounds[None, :]).astype(jnp.int32), axis=1)
    key_doc = jnp.sum((key_pos[:, None] >= bounds[None, :]).astype(jnp.int32), axis=1)
    causal = (key_pos[None, :] <= query_pos[:, None]) & (key_pos[None, :] >= 0)
    return causal & (key_doc[None, :] == query_doc[:, None])


def attend(queries, keys, values, allowed):
    row_count, channels = queries.shape
    heads = channels // HEAD

    def split_heads(matrix):
        return matrix.reshape(matrix.shape[0], heads, HEAD).transpose(1, 0, 2)

    def one_head(head_parts):
        query_rows, key_rows, value_rows = head_parts
        scores = jnp.dot(query_rows, key_rows.T, preferred_element_type=jnp.float32) * (
            1.0 / math.sqrt(HEAD)
        )
        scores = jnp.where(allowed, scores, -jnp.inf)
        row_max = jnp.max(scores, axis=1, keepdims=True)
        exp_scores = jnp.exp(scores - row_max)
        weight = (exp_scores / jnp.sum(exp_scores, axis=1, keepdims=True)).astype(jnp.bfloat16)
        return jnp.dot(weight, value_rows, preferred_element_type=jnp.float32).astype(jnp.bfloat16)

    head_out = lax.map(one_head, (split_heads(queries), split_heads(keys), split_heads(values)))
    return head_out.transpose(1, 0, 2).reshape(row_count, channels)


def on_device(hyena_qkv, short_weight, filter_rate, filter_residue, attn_qkv, doc_lengths):
    row_count = hyena_qkv.shape[0]
    channels = hyena_qkv.shape[2]
    groups = filter_rate.shape[0]
    device_index = lax.axis_index("ctx")
    before = from_behind(hyena_qkv[row_count - 2 :], "ctx", 1)
    featured = featurize(hyena_qkv, before, short_weight)
    mixed_in = (featured[:, 1] * featured[:, 2]).astype(jnp.bfloat16)
    mode_coeff, filter_taps = filter_terms(filter_rate, filter_residue, row_count)
    grouped = mixed_in.reshape(row_count, groups, channels // groups)
    near_part = jnp.einsum(
        "gts,sgc->tgc", toeplitz(filter_taps), grouped, preferred_element_type=jnp.float32
    )
    end_states = block_ends(mixed_in, filter_rate)
    pieces = lax.all_gather(end_states[None], "ctx", axis=0, tiled=True)
    owners = jnp.arange(pieces.shape[0], dtype=jnp.int32)
    absorb_distance = device_index - 1 - owners
    lag_values = (jnp.maximum(absorb_distance, 0) * row_count).astype(jnp.float32)
    powers = jnp.exp(-filter_rate[None] * lag_values[:, None, None])
    powers = jnp.where((absorb_distance >= 0)[:, None, None], powers, 0.0)
    carried = jnp.einsum("ngm,ngmc->gmc", powers, pieces, precision=precise)
    far_part = block_far(carried, filter_rate, mode_coeff, row_count)
    hyena_out = (featured[:, 0] * (near_part + far_part).reshape(row_count, channels)).astype(
        jnp.bfloat16
    )
    key_pairs = attn_qkv[:, 1:]
    key_blocks = [key_pairs]
    moving = key_pairs
    for distance in range(1, SPAN):
        moving = from_behind(moving, "ctx", 1)
        key_blocks.append(moving)
    window = jnp.concatenate(key_blocks[::-1], axis=0)
    query_pos = device_index * row_count + jnp.arange(row_count, dtype=jnp.int32)
    key_pos = (device_index - SPAN + 1) * row_count + jnp.arange(SPAN * row_count, dtype=jnp.int32)
    allowed = visible(query_pos, key_pos, doc_lengths)
    attn_out = attend(attn_qkv[:, 0], window[:, 0], window[:, 1], allowed)
    return (hyena_out, attn_out)


LANES = 128
PLANE = 4
EDGE = 16


def fused_kernel(
    n,
    hq_hbm,
    short_hbm,
    rate_hbm,
    residue_hbm,
    docs_hbm,
    aq,
    hyena_out,
    attn_out,
    hq,
    short_weight,
    rate_t,
    residue_t,
    docs,
    gath,
    obuf,
    prev,
    mixed,
    rate_rows,
    coeff_rows,
    near,
    far_powers,
    rate_c,
    own_state,
    state_send,
    state_in,
    total_send,
    total_in,
    sem_q_send,
    sem_q_recv,
    sem_o_send,
    sem_o_recv,
    sem_edge,
    sem_s_send,
    sem_s_recv,
    sem_t_send,
    sem_t_recv,
    sem_in,
):
    rows = hq.shape[1]
    modes = rate_t.shape[0]
    groups = rate_t.shape[1]
    channels = hq.shape[2]
    width = channels // groups
    per_tile = LANES // width
    tiles = channels // LANES
    planes = n // PLANE
    me = lax.axis_index("ctx")
    plane = me // PLANE
    spot = lax.rem(me, PLANE)

    def remote(src, dst, send_sem, recv_sem, target):
        return pltpu.make_async_remote_copy(
            src_ref=src,
            dst_ref=dst,
            send_sem=send_sem,
            recv_sem=recv_sem,
            device_id={"ctx": target},
            device_id_type=pl.DeviceIdType.MESH,
        )

    def head_columns(h):
        return pl.ds(pl.multiple_of(h * HEAD, HEAD), HEAD)

    def send_head(h, slot):
        return remote(
            aq.at[:, :, head_columns(h)],
            gath.at[slot + pad],
            sem_q_send.at[h],
            sem_q_recv.at[slot],
            h,
        )

    def send_out(b, slot):
        return remote(
            obuf.at[b],
            attn_out.at[:, head_columns(slot)],
            sem_o_send.at[b],
            sem_o_recv.at[slot],
            b,
        )

    def send_edge():
        return remote(
            hq_hbm.at[:, pl.ds(rows - EDGE, EDGE), :],
            prev,
            sem_edge.at[0],
            sem_edge.at[1],
            lax.rem(me + 1, n),
        )

    def send_state(target_spot, slot):
        return remote(
            state_send,
            state_in.at[slot],
            sem_s_send.at[target_spot],
            sem_s_recv.at[slot],
            plane * PLANE + target_spot,
        )

    def send_total(target_plane, slot):
        return remote(
            total_send,
            total_in.at[slot],
            sem_t_send.at[target_plane],
            sem_t_recv.at[slot],
            target_plane * PLANE + spot,
        )

    loads = [
        pltpu.make_async_copy(source, target, sem_in.at[k])
        for k, (source, target) in enumerate(
            (
                (hq_hbm, hq),
                (short_hbm, short_weight),
                (rate_hbm, rate_t),
                (residue_hbm, residue_t),
                (docs_hbm, docs),
            )
        )
    ]
    for load in loads:
        load.start()

    barrier = pltpu.get_barrier_semaphore()

    @pl.loop(1, n)
    def _(k):
        pl.semaphore_signal(
            barrier,
            inc=1,
            device_id={"ctx": lax.rem(me + k, n)},
            device_id_type=pl.DeviceIdType.MESH,
        )

    pl.semaphore_wait(barrier, n - 1)

    @pl.when(me < n - 1)
    def _():
        send_edge().start()

    early = n // 2
    pad = min(SPAN, n) - 1

    @pl.loop(1, early)
    def _(k):
        send_head(lax.rem(me + n - k, n), me).start()

    own_heads = pltpu.make_async_copy(
        aq.at[:, :, head_columns(me)], gath.at[me + pad], sem_q_recv.at[me]
    )
    own_heads.start()

    for p in range(pad):
        gath[p] = jnp.zeros(gath.shape[1:], gath.dtype)

    @pl.when(me == 0)
    def _():
        prev[...] = jnp.zeros_like(prev)

    @pl.when(me > 0)
    def _():
        send_edge().wait_recv()

    for load in loads:
        load.wait()

    lane = lax.broadcasted_iota(jnp.int32, (1, LANES), 1)
    sub = lax.broadcasted_iota(jnp.int32, (LANES, 1), 0)
    own_block = (sub // width) == (lane // width)
    row_col = lax.broadcasted_iota(jnp.int32, (rows, 1), 0)
    row_f = row_col.astype(jnp.float32)
    key_row = lax.broadcasted_iota(jnp.int32, (1, rows), 1)
    lower = key_row <= row_col
    mode_pick = lax.broadcasted_iota(jnp.int32, (modes, 1), 0) == lax.rem(lane, modes)
    rev_f = lax.rem(rows - row_col, rows).astype(jnp.float32)
    filter_of = (
        lax.broadcasted_iota(jnp.int32, (per_tile, 1), 0) == lane // width
    ).astype(jnp.float32)

    def feature_at(j, at):
        value = jnp.concatenate([prev[j, :, at], hq[j, :, at]], axis=0).astype(jnp.float32)
        one = pltpu.roll(value, 1, 0)
        two = pltpu.roll(value, 2, 0)
        return (
            short_weight[0, pl.ds(j, 1), at] * value[EDGE:]
            + short_weight[1, pl.ds(j, 1), at] * one[EDGE:]
            + short_weight[2, pl.ds(j, 1), at] * two[EDGE:]
        )

    @pl.loop(0, tiles)
    def _(i):
        at = pl.ds(pl.multiple_of(i * LANES, LANES), LANES)

        def feature(j):
            return feature_at(j, at)

        mixed_f = feature(1) * feature(2)
        mixed_b = mixed_f.astype(jnp.bfloat16)
        mixed_in = mixed_b.astype(jnp.float32)

        pick = (
            lax.broadcasted_iota(jnp.int32, (groups, LANES), 0)
            == i * per_tile + lane // width
        ).astype(jnp.float32)
        rates = jnp.dot(rate_t[...], pick, precision=precise, preferred_element_type=jnp.float32)
        residues = jnp.dot(
            residue_t[...], pick, precision=precise, preferred_element_type=jnp.float32
        )
        coeffs = residues * jnp.sqrt(2.0 * rates / modes)
        rate_c[:, at] = rates
        rate_row = jnp.sum(jnp.where(mode_pick, rates, 0.0), axis=0, keepdims=True)
        coeff_row = jnp.sum(jnp.where(mode_pick, coeffs, 0.0), axis=0, keepdims=True)

        ends = jnp.exp(-rate_row * (rows - 1 - row_f))
        full = lax.dot_general(
            ends,
            mixed_in,
            (((0,), (0,)), ((), ())),
            precision=precise,
            preferred_element_type=jnp.float32,
        )
        full = jnp.where(own_block, full, 0.0).reshape(per_tile, modes, LANES)
        state = jnp.sum(full, axis=0)
        own_state[:, at] = state
        state_send[:, at] = state.astype(jnp.bfloat16)
        far_powers[:, at] = coeff_row * jnp.exp(-rate_row * (row_f + 1.0))

        mixed[:, at] = mixed_b
        rate_rows[:, at] = jnp.broadcast_to(rate_row, (8, LANES))
        coeff_rows[:, at] = jnp.broadcast_to(coeff_row, (8, LANES))

    for other in range(PLANE):

        @pl.when(spot != other)
        def _(other=other):
            send_state(other, spot).start()

    @pl.loop(early, n)
    def _(k):
        send_head(lax.rem(me + n - k, n), me).start()

    def near_tile(i):
        at = pl.ds(pl.multiple_of(i * LANES, LANES), LANES)
        mixed_in = mixed[:, at].astype(jnp.float32)
        rate_row = rate_rows[pl.ds(0, 1), at]
        coeff_row = coeff_rows[pl.ds(0, 1), at]
        taps_powers = coeff_row * jnp.exp(-rate_row * rev_f)
        taps = lax.dot_general(
            filter_of,
            taps_powers,
            (((1,), (1,)), ((), ())),
            precision=precise,
            preferred_element_type=jnp.float32,
        )
        tables = []
        inputs = []
        for g in range(per_tile):
            spread = jnp.broadcast_to(taps[g : g + 1, :], (rows, rows))
            table = pltpu.roll(spread, 0, 1, stride=1, stride_axis=0)
            tables.append(jnp.where(lower, table, 0.0).astype(jnp.bfloat16))
            inputs.append(jnp.where(lane // width == g, mixed_in, 0.0).astype(jnp.bfloat16))
        near[:, at] = jnp.dot(
            jnp.concatenate(tables, axis=1),
            jnp.concatenate(inputs, axis=0),
            preferred_element_type=jnp.float32,
        )

    first_tiles = (tiles * 16) // 16

    @pl.loop(0, first_tiles)
    def _(i):
        near_tile(i)

    def decay(steps):
        return jnp.exp(rate_c[...] * (-float(rows) * steps.astype(jnp.float32)))

    own_state[...] = decay(PLANE - 1 - spot) * own_state[...]
    for other in range(PLANE):

        @pl.when(spot != other)
        def _(other=other):
            send_state(other, other).wait_recv()
            own_state[...] += decay(jnp.int32(PLANE - 1 - other)) * state_in[other].astype(
                jnp.float32
            )

    total_send[...] = own_state[...].astype(jnp.bfloat16)
    for later in range(planes):

        @pl.when(plane < later)
        def _(later=later):
            send_total(later, plane).start()

    bounds = []
    running = jnp.int32(0)
    for k in range(docs.shape[0]):
        running = running + docs[k]
        bounds.append(running)
    scale = 1.0 / math.sqrt(HEAD)
    span = min(SPAN, n)
    head_row = lax.broadcasted_iota(jnp.int32, (rows, 1), 0)
    window_row = lax.broadcasted_iota(jnp.int32, (1, span * rows), 1)

    def attend_block(b):
        begin = b - pad
        keys = gath[pl.ds(b, span), 1].reshape(span * rows, HEAD)
        values = gath[pl.ds(b, span), 2].reshape(span * rows, HEAD)
        scores = lax.dot_general(
            gath[b + pad, 0], keys, (((1,), (1,)), ((), ())), preferred_element_type=jnp.float32
        )
        query_pos = b * rows + head_row
        first = jnp.zeros_like(query_pos)
        for bound in bounds:
            first = jnp.where(query_pos >= bound, bound, first)
        key_pos = begin * rows + window_row
        allowed = (key_pos <= query_pos) & (key_pos >= first)
        scores = jnp.where(allowed, scores, -jnp.inf)
        row_max = jnp.max(scores, axis=1, keepdims=True)
        exp_scores = jnp.exp((scores - row_max) * scale)
        row_sum = jnp.sum(exp_scores, axis=1, keepdims=True)
        mixed_values = jnp.dot(
            exp_scores.astype(jnp.bfloat16), values, preferred_element_type=jnp.float32
        )
        obuf[b] = (mixed_values / row_sum).astype(jnp.bfloat16)

        @pl.when(b != me)
        def _():
            send_out(b, me).start()

        @pl.when(b == me)
        def _():
            pltpu.make_async_copy(
                obuf.at[b], attn_out.at[:, head_columns(me)], sem_o_recv.at[me]
            ).start()

    own_heads.wait()

    @pl.loop(1, span)
    def _(k):
        source = lax.rem(me + k, n)
        send_head(source, source).wait_recv()

    @pl.loop(0, n)
    def _(i):
        b = lax.rem(me + span + i, n)

        @pl.when(i < n - span)
        def _():
            send_head(b, b).wait_recv()

        attend_block(b)

    @pl.loop(first_tiles, tiles)
    def _(i):
        near_tile(i)

    own_state[...] = jnp.zeros(own_state.shape, jnp.float32)
    for earlier in range(planes):

        @pl.when(earlier < plane)
        def _(earlier=earlier):
            send_total(earlier, earlier).wait_recv()
            steps = PLANE * (plane - 1 - earlier) + spot
            own_state[...] += decay(steps) * total_in[earlier].astype(jnp.float32)

    for other in range(PLANE):

        @pl.when(other < spot)
        def _(other=other):
            own_state[...] += decay(spot - 1 - other) * state_in[other].astype(jnp.float32)

    @pl.loop(0, tiles)
    def _(i):
        at = pl.ds(pl.multiple_of(i * LANES, LANES), LANES)
        carried = jnp.concatenate([own_state[:, at]] * per_tile, axis=0)
        carried = jnp.where(own_block, carried, 0.0)
        far = jnp.dot(
            far_powers[:, at], carried, precision=precise, preferred_element_type=jnp.float32
        )
        hyena_out[:, at] = (feature_at(0, at) * (near[:, at] + far)).astype(jnp.bfloat16)

    @pl.when(me < n - 1)
    def _():
        send_edge().wait_send()

    for other in range(PLANE):

        @pl.when(spot != other)
        def _(other=other):
            send_state(other, spot).wait_send()

    for later in range(planes):

        @pl.when(plane < later)
        def _(later=later):
            send_total(later, plane).wait_send()

    @pl.loop(0, n)
    def _(b):
        @pl.when(b != me)
        def _():
            send_head(b, me).wait_send()
            send_out(b, me).wait_send()
            send_out(b, b).wait_recv()

        @pl.when(b == me)
        def _():
            pltpu.make_async_copy(
                obuf.at[b], attn_out.at[:, head_columns(me)], sem_o_recv.at[me]
            ).wait()


def by_heads(n, hyena_qkv, short_weight, filter_rate, filter_residue, attn_qkv, doc_lengths):
    rows, streams, channels = hyena_qkv.shape
    modes = filter_rate.shape[1]
    out = jax.ShapeDtypeStruct((rows, channels), jnp.bfloat16)
    vmem = pl.BlockSpec(memory_space=pltpu.VMEM)
    dma = pltpu.SemaphoreType.DMA
    bf16, f32 = jnp.bfloat16, jnp.float32
    return pl.pallas_call(
        functools.partial(fused_kernel, n),
        out_shape=(out, out),
        in_specs=[pl.BlockSpec(memory_space=pltpu.HBM)] * 6,
        out_specs=(vmem, vmem),
        scratch_shapes=[
            pltpu.VMEM((streams, rows, channels), bf16),
            pltpu.VMEM(short_weight.shape, f32),
            pltpu.VMEM(filter_rate.T.shape, f32),
            pltpu.VMEM(filter_rate.T.shape, f32),
            pltpu.SMEM(doc_lengths.shape, jnp.int32),
            pltpu.VMEM((n + min(SPAN, n) - 1, streams, rows, HEAD), bf16),
            pltpu.VMEM((n, rows, HEAD), bf16),
            pltpu.VMEM((streams, EDGE, channels), bf16),
            pltpu.VMEM((rows, channels), bf16),
            pltpu.VMEM((8, channels), f32),
            pltpu.VMEM((8, channels), f32),
            pltpu.VMEM((rows, channels), f32),
            pltpu.VMEM((rows, channels), f32),
            pltpu.VMEM((modes, channels), f32),
            pltpu.VMEM((modes, channels), f32),
            pltpu.VMEM((modes, channels), bf16),
            pltpu.VMEM((PLANE, modes, channels), bf16),
            pltpu.VMEM((modes, channels), bf16),
            pltpu.VMEM((n // PLANE, modes, channels), bf16),
            dma((n,)),
            dma((n,)),
            dma((n,)),
            dma((n,)),
            dma((2,)),
            dma((PLANE,)),
            dma((PLANE,)),
            dma((n // PLANE,)),
            dma((n // PLANE,)),
            dma((5,)),
        ],
        compiler_params=pltpu.CompilerParams(
            collective_id=0, has_side_effects=True, vmem_limit_bytes=48 * 2**20
        ),
    )(
        hyena_qkv.transpose(1, 0, 2),
        short_weight,
        filter_rate.T,
        filter_residue.T,
        doc_lengths,
        attn_qkv.transpose(1, 0, 2),
    )


def on_any_slice(hyena_qkv, short_weight, filter_rate, filter_residue, attn_qkv, doc_lengths):
    n = lax.axis_size("ctx")
    rows, _, channels = hyena_qkv.shape
    groups, modes = filter_rate.shape
    fits = (
        channels == n * HEAD
        and n % PLANE == 0
        and channels == groups * modes
        and LANES % modes == 0
        and rows == LANES
    )
    args = (hyena_qkv, short_weight, filter_rate, filter_residue, attn_qkv, doc_lengths)
    return by_heads(n, *args) if fits else on_device(*args)


def solution(mesh):
    in_specs = (
        P(("group", "ctx"), None, None),
        P(),
        P(),
        P(),
        P(("group", "ctx"), None, None),
        P("group"),
    )
    out_specs = (P(("group", "ctx"), None), P(("group", "ctx"), None))
    return jax.shard_map(
        on_any_slice, mesh=mesh, in_specs=in_specs, out_specs=out_specs, check_vma=False
    )
```
